32 devices in a mesh: grp: 2 (over y), seq: 4 (over z), chan: 4 (over x, core).
Axes of the slice: x: 2, y: 2, z: 4, core: 2. Of those that a mesh axis runs over, the one named last changes fastest.
Arguments:
- inputs: bfloat16 [4, 1024, 1536], P('grp', 'seq', 'chan'), parts along dimension 0, may hold values from -30 to 30, as said below
- cotangent: bfloat16 [4, 1024, 1536], P('grp', 'seq', 'chan'), parts along dimension 0, may hold values from -6 to 6
- dilated_weight: bfloat16 [3, 1536, 768], P(None, None, 'chan'), may hold values from -0.09375 to 0.09375
- w_point: bfloat16 [1536, 768], P(None, 'chan'), may hold values from -0.21875 to 0.21875
- norm_gain: float32 [1536], replicated, may hold values from 0.1 to 1.9
Outputs:
- input_grad: bfloat16 [4, 1024, 1536], P('grp', 'seq', 'chan'), parts along dimension 0
- point_grad: float32 [3072, 768], P(('grp', 'seq'), 'chan'), parts along dimension 0
The draws below stay inside these ranges and needn't reach their ends.
There are 2 independent parts, one for each index of `grp`. The reference program is written for one: setup_inputs(seed, part) draws one part's arguments, and reference() takes and returns one part's arrays. A program takes and returns all parts, laid end to end along the dimension named above; an argument that names none is the same for every part. Nothing has to cross between parts.
Inputs may be any that keep to these rules, and one draw needn't show every extreme that they name: `inputs`: the block's input activations.
All inputs are finite; a program needn't handle non-finite values.
Results may differ from the reference program's by a relative error of at most 0.007.
Values may be sent and summed in bfloat16 or wider, within the bound.
A program may use at most 64 MiB of HBM per device.

```python
import math
import jax
import jax.numpy as jnp
from jax import lax

C = 1536
H = 768
BATCH = 2
DILATION_STEP = 512
LENGTH = 1024
N_CHAN = 4


column_norm = math.sqrt(2.0 * math.log(10.0) / 99.0)


def draw_inputs(key, part):
    keys = jax.random.split(key, 3)
    shape = (BATCH, LENGTH, C)
    columns = jnp.exp(jax.random.uniform(keys[2], (1, 1, C), jnp.float32, 0.0, math.log(10.0))) * column_norm
    base = jnp.clip(jax.random.normal(keys[0], shape, jnp.float32), -4.0, 4.0)
    rows = jnp.exp(jax.random.uniform(keys[1], (BATCH, LENGTH, 1), jnp.float32, math.log(0.3), math.log(3.0)))
    return (base * rows * columns).astype(jnp.bfloat16)


def strengthened(result, rng, source, target, blocks, factor):
    owner, partner = [(jnp.arange(result.shape[dim]) // (result.shape[dim] // blocks)).reshape([-1 if axis == dim else 1 for axis in range(result.ndim)]) for dim in (source, target)]
    chosen = jax.random.permutation(rng, blocks)[partner]
    strong = (owner == chosen) | (owner == (partner + blocks // 2) % blocks)
    return jnp.where(strong, factor * result, result)


def shard_levels(key, extent, pieces, least, high):
    def one(axis_at, parts):
        steps = jax.random.uniform(jax.random.fold_in(jax.random.fold_in(key, 6), axis_at), (parts,), jnp.float32, least / len(pieces), high / len(pieces))
        return jnp.repeat(jnp.exp(steps), extent[axis_at] // parts).reshape((-1,) + (1,) * (len(extent) - axis_at - 1))

    factor_of = one(*pieces[0])
    for cut in pieces[1:]:
        factor_of = factor_of * one(*cut)
    return factor_of


def noise(stream_key, shape, deviation, bound, cuts=(), kind=jnp.bfloat16):
    gain = shard_levels(stream_key, shape, cuts, -0.22, 0.18) if cuts else 1.0
    drawn = jax.random.normal(stream_key, shape, jnp.float32) * deviation * gain
    return jnp.minimum(jnp.maximum(drawn, -bound), bound).astype(kind)


def bell_draw_with(rng, shape, spread, bound, cuts, heavy, kind=jnp.bfloat16):
    drawn = spread * jax.random.normal(rng, shape, jnp.float32)
    if cuts:
        drawn = drawn * shard_levels(rng, shape, cuts, -0.22, 0.18)
    return jnp.clip(strengthened(drawn, jax.random.fold_in(rng, 3), *heavy), -bound, bound).astype(kind)


def setup_inputs(seed: int = 0, part: int = 0) -> dict:
    splits = jax.random.split(jax.random.key(seed), 6)
    part_keys = jax.random.split(jax.random.fold_in(splits[5], part), 6)
    inputs = draw_inputs(jax.random.fold_in(jax.random.fold_in(splits[5], part), 71), part)
    cotangent = bell_draw_with(part_keys[1], (BATCH, LENGTH, C), 1.0, 6.0, ((1, 4), (2, 4)), (1, 2, 4, 2.0))
    dilated_weight = noise(splits[2], (3, C, H), (3 * C) ** -0.5, 0.09375, ((2, 4),))
    w_point = noise(splits[3], (C, H), H ** -0.5, 0.21875, ((1, 4),))
    norm_gain = jnp.clip(1.0 + 0.18 * jax.random.normal(splits[4], (C,), jnp.float32), 0.1, 1.9)
    return {"inputs": inputs, "cotangent": cotangent, "dilated_weight": dilated_weight, "w_point": w_point, "norm_gain": norm_gain}


epsilon = 1e-05

def gelu_value(values):
    return 0.5 * values * (1.0 + lax.erf(values * (1.0 / math.sqrt(2.0))))

def gelu_slope(values):
    return 0.5 * (1.0 + lax.erf(values * (1.0 / math.sqrt(2.0)))) + values * jnp.exp(-0.5 * values * values) * (1.0 / math.sqrt(2.0 * math.pi))

def shifted_rows(values, offset):
    padding = jnp.zeros((values.shape[0], abs(offset), values.shape[2]), values.dtype)
    if offset > 0:
        return jnp.concatenate([padding, values[:, :-offset]], axis=1)
    return jnp.concatenate([values[:, -offset:], padding], axis=1)

def forward_tap_rows(values, weights):
    return jnp.einsum('bpc,ch->bph', values.astype(jnp.float32), weights.astype(jnp.float32))

def backward_tap(values, weights):
    return jnp.einsum('bph,ch->bpc', values.astype(jnp.float32), weights.astype(jnp.float32))

def reference(inputs, cotangent, dilated_weight, w_point, norm_gain):
    signal = inputs.astype(jnp.float32)
    row_scale = lax.rsqrt(lax.optimization_barrier(jnp.mean(signal * signal, axis=-1, keepdims=True)) + epsilon)
    normed = signal * row_scale * norm_gain
    hidden_state = gelu_value(normed).astype(jnp.bfloat16)
    dilated_output = forward_tap_rows(shifted_rows(hidden_state, DILATION_STEP), dilated_weight[0]) + forward_tap_rows(hidden_state, dilated_weight[1]) + forward_tap_rows(shifted_rows(hidden_state, -DILATION_STEP), dilated_weight[2])
    activated = gelu_value(dilated_output).astype(jnp.bfloat16)
    hidden_grad = jnp.einsum('bpc,ch->bph', cotangent.astype(jnp.float32), w_point.astype(jnp.float32))
    dilated_output_grad = (hidden_grad * gelu_slope(dilated_output)).astype(jnp.bfloat16)
    gradient_after = shifted_rows(dilated_output_grad, -DILATION_STEP)
    gradient_before = shifted_rows(dilated_output_grad, DILATION_STEP)
    group_width = H // N_CHAN
    normed_grad = jnp.zeros(signal.shape, jnp.float32)
    for group in range(N_CHAN):
        first = group * group_width
        last = first + group_width
        partial_sum = backward_tap(gradient_after[:, :, first:last], dilated_weight[0][:, first:last])
        partial_sum = partial_sum + backward_tap(dilated_output_grad[:, :, first:last], dilated_weight[1][:, first:last])
        partial_sum = partial_sum + backward_tap(gradient_before[:, :, first:last], dilated_weight[2][:, first:last])
        rounded = lax.optimization_barrier(partial_sum.astype(jnp.bfloat16))
        normed_grad = normed_grad + rounded.astype(jnp.float32)
    scaled_grad = normed_grad * gelu_slope(normed) * norm_gain
    unit = signal * row_scale
    inner_mean = lax.optimization_barrier(jnp.mean(scaled_grad * unit, axis=-1, keepdims=True))
    input_grad = (cotangent.astype(jnp.float32) + row_scale * (scaled_grad - unit * inner_mean)).astype(jnp.bfloat16)
    point_grad = jnp.einsum('bpc,bph->ch', cotangent.astype(jnp.float32), activated.astype(jnp.float32))
    return (input_grad, point_grad)
```

```python
import math

import jax
import jax.numpy as jnp
from jax import lax
from jax.sharding import PartitionSpec as P

DILATION_STEP = 512


epsilon = 1e-05


def passed_along(block, axis, distance):
    devices = range(lax.axis_size(axis))
    route = [(i - distance, i) for i in devices if i - distance in devices]
    return lax.ppermute(block, axis, route)


def gelu_value(values):
    return 0.5 * values * (1.0 + lax.erf(values * (1.0 / math.sqrt(2.0))))


def gelu_slope(values):
    return 0.5 * (1.0 + lax.erf(values * (1.0 / math.sqrt(2.0)))) + values * jnp.exp(
        -0.5 * values * values
    ) * (1.0 / math.sqrt(2.0 * math.pi))


def activate(whole_input, norm_gain):
    signal = whole_input.astype(jnp.float32)
    row_scale = lax.rsqrt(jnp.mean(signal * signal, axis=-1, keepdims=True) + epsilon)
    return (gelu_value(signal * row_scale * norm_gain).astype(jnp.bfloat16), row_scale)


def forward_tap_rows(values, weights):
    return jnp.einsum("bpc,ch->bph", values, weights, preferred_element_type=jnp.float32)


def backward_tap(values, weights):
    return jnp.einsum("bph,ch->bpc", values, weights, preferred_element_type=jnp.float32)


def per_device(inputs, cotangent, dilated_weight, w_point, norm_gain):
    stride_dev = DILATION_STEP // inputs.shape[1]
    whole_input, whole_grad = (
        lax.all_gather(inputs, "chan", axis=2, tiled=True),
        lax.all_gather(cotangent, "chan", axis=2, tiled=True),
    )
    hidden_state, row_scale = activate(whole_input, norm_gain)
    behind = passed_along(
        forward_tap_rows(hidden_state, dilated_weight[0]).astype(jnp.bfloat16), "seq", stride_dev
    )
    onward = passed_along(
        forward_tap_rows(hidden_state, dilated_weight[2]).astype(jnp.bfloat16), "seq", -stride_dev
    )
    dilated_output = (
        behind.astype(jnp.float32)
        + forward_tap_rows(hidden_state, dilated_weight[1])
        + onward.astype(jnp.float32)
    )
    activated = gelu_value(dilated_output).astype(jnp.bfloat16)
    hidden_grad = forward_tap_rows(whole_grad, w_point)
    dilated_output_grad = (hidden_grad * gelu_slope(dilated_output)).astype(jnp.bfloat16)
    gradient_after = passed_along(dilated_output_grad, "seq", -stride_dev)
    gradient_before = passed_along(dilated_output_grad, "seq", stride_dev)
    partial_grad = (
        backward_tap(gradient_after, dilated_weight[0])
        + backward_tap(dilated_output_grad, dilated_weight[1])
        + backward_tap(gradient_before, dilated_weight[2])
    )
    chan_width = inputs.shape[2]
    chan_index = lax.axis_index("chan")
    channels = norm_gain.shape[0]
    normed_grad = lax.psum_scatter(
        partial_grad.astype(jnp.bfloat16), "chan", scatter_dimension=2, tiled=True
    ).astype(jnp.float32)
    local_gain = lax.dynamic_slice_in_dim(norm_gain, chan_index * chan_width, chan_width)
    signal = inputs.astype(jnp.float32)
    unit = signal * row_scale
    scaled_grad = normed_grad * gelu_slope(unit * local_gain) * local_gain
    norm_total = lax.psum(jnp.sum(scaled_grad * unit, axis=-1, keepdims=True), "chan")
    branch_grad = row_scale * (scaled_grad - unit * (norm_total / channels))
    input_grad = (cotangent.astype(jnp.float32) + branch_grad).astype(jnp.bfloat16)
    flat_grad = whole_grad.reshape(-1, channels)
    flat_active = activated.reshape(-1, activated.shape[2])
    point_grad = lax.psum_scatter(
        lax.dot_general(
            flat_grad, flat_active, (((0,), (0,)), ((), ())), preferred_element_type=jnp.float32
        ),
        "seq",
        scatter_dimension=0,
        tiled=True,
    )
    return (input_grad, point_grad)


def solution(mesh):
    placed = (
        P("grp", "seq", "chan"),
        P("grp", "seq", "chan"),
        P(None, None, "chan"),
        P(None, "chan"),
        P(),
    )
    return jax.shard_map(
        per_device,
        mesh=mesh,
        in_specs=placed,
        out_specs=(P("grp", "seq", "chan"), P(("grp", "seq"), "chan")),
        check_vma=False,
    )
```

```python
import functools
import math

import jax
import jax.numpy as jnp
from jax import lax
from jax.experimental import pallas as pl
from jax.experimental.pallas import tpu as pltpu
from jax.sharding import PartitionSpec as P

DILATION_STEP = 512
epsilon = 1e-05
N_SEMS = 64
F32 = jnp.float32
BF16 = jnp.bfloat16
MESH = pl.DeviceIdType.MESH


def gelu_value(values):
    return 0.5 * values * (1.0 + lax.erf(values * (1.0 / math.sqrt(2.0))))


def gelu_slope(values):
    return 0.5 * (1.0 + lax.erf(values * (1.0 / math.sqrt(2.0)))) + values * jnp.exp(
        -0.5 * values * values
    ) * (1.0 / math.sqrt(2.0 * math.pi))


def dot_nn(a, b):
    return lax.dot_general(a, b, (((1,), (0,)), ((), ())), preferred_element_type=F32)


def dot_nt(a, b):
    return lax.dot_general(a, b, (((1,), (1,)), ((), ())), preferred_element_type=F32)


def dot_tn(a, b):
    return lax.dot_general(a, b, (((0,), (0,)), ((), ())), preferred_element_type=F32)


def lanes_to_row(values):
    total = values[:, 0:128]
    for at in range(128, values.shape[1], 128):
        total = total + values[:, at : at + 128]
    return jnp.sum(total.T, axis=0, keepdims=True)


def row_to_columns(row):
    return jnp.broadcast_to(row, (128, 128)).T


def widen(columns, width):
    return jnp.concatenate([columns] * (width // 128), axis=1)


def kernel(
    seq_n, stride, scatter, x_ref, ct_ref, w_ref, wp_ref, gain_ref, out_ref, pg_ref,
    hid, cot, ss, rs, slope, dil, acc_lo, acc_hi, act, hg, y_lo, y_hi, yr_lo, yr_hi, dg, dr_lo, dr_hi,
    part, ps, pr, xs, xr, sg, pn, qs, qr, qs2, qr2, send_sem, recv_sem,
):
    batch, rows, width = x_ref.shape
    channels = gain_ref.shape[1]
    c = lax.axis_index("chan")
    s = lax.axis_index("seq")
    c1 = c + 1 - 2 * lax.rem(c, 2)
    c2 = lax.rem(c + 2, 4)
    c3 = 3 - c
    peers = (c, c1, c2, c3)
    s1 = s + 1 - 2 * lax.rem(s, 2)
    s2 = lax.rem(s + 2, 4)
    s3 = 3 - s
    has_hi = s + stride < seq_n
    has_lo = s >= stride
    up = lax.rem(s + stride, seq_n)
    down = lax.rem(s - stride + seq_n, seq_n)

    count = [0]
    sent = []

    def copy(src, dst, device):
        k = count[0]
        count[0] += 1
        return pltpu.make_async_remote_copy(
            src_ref=src, dst_ref=dst, send_sem=send_sem.at[k], recv_sem=recv_sem.at[k],
            device_id=device, device_id_type=MESH,
        )

    def push(src, dst, device):
        handle = copy(src, dst, device)
        handle.start()
        sent.append(handle)
        return handle

    def chan_rows(ch):
        return pl.ds(pl.multiple_of(ch * width, width), width)

    barrier = pltpu.get_barrier_semaphore()
    for peer in (c1, c2, c3):
        pl.semaphore_signal(barrier, inc=1, device_id={"chan": peer}, device_id_type=MESH)

    @pl.when(has_hi)
    def _():
        pl.semaphore_signal(barrier, inc=1, device_id={"seq": up}, device_id_type=MESH)

    @pl.when(has_lo)
    def _():
        pl.semaphore_signal(barrier, inc=1, device_id={"seq": down}, device_id_type=MESH)

    if scatter:
        pl.semaphore_signal(barrier, inc=1, device_id={"seq": s1}, device_id_type=MESH)

    for b in range(batch):
        for at in range(0, rows, 128):
            v = x_ref[b, at : at + 128, :].astype(F32)
            ss[0, :, b * rows + at : b * rows + at + 128] = jnp.broadcast_to(lanes_to_row(v * v), (8, 128))

    cot[c] = ct_ref[...]
    ways = has_hi.astype(jnp.int32) + has_lo.astype(jnp.int32)
    pl.semaphore_wait(barrier, ways + (4 if scatter else 3))

    ss_in = [push(ss.at[0], ss.at[k], {"chan": peers[k]}) for k in (2, 3, 1)]
    cot_in = [[None] * batch for _ in range(4)]
    hid_in = [[None] * batch for _ in range(4)]

    def spread_cot(b):
        cot_in[2][b] = push(cot.at[c, b], cot.at[c, b], {"chan": c2})
        cot_in[1][b] = push(cot.at[c, b], cot.at[c, b], {"chan": c1})

    def relay_cot(b):
        copy_in = cot_in[2][b]
        copy_in.wait_recv()
        cot_in[3][b] = push(cot.at[c2, b], cot.at[c2, b], {"chan": c1})

    spread_cot(0)
    for handle in ss_in:
        handle.wait_recv()
    gain = gain_ref[:, chan_rows(c)]
    for b in range(batch):
        for at in range(0, rows, 128):
            here = slice(b * rows + at, b * rows + at + 128)
            total = ss[0, 0:1, here] + ss[1, 0:1, here] + ss[2, 0:1, here] + ss[3, 0:1, here]
            columns = row_to_columns(lax.rsqrt(total * (1.0 / channels) + epsilon))
            rs[b, at : at + 128, :] = columns
            normed = x_ref[b, at : at + 128, :].astype(F32) * widen(columns, width) * gain
            hid[0, b, at : at + 128, :] = gelu_value(normed).astype(BF16)
        hid_in[2][b] = push(hid.at[0, b], hid.at[2, b], {"chan": c2})
        hid_in[1][b] = push(hid.at[0, b], hid.at[1, b], {"chan": c1})
    for b in range(1, batch):
        spread_cot(b)

    def normed_slope(b):
        for at in range(0, rows, 128):
            normed = x_ref[b, at : at + 128, :].astype(F32) * widen(rs[b, at : at + 128, :], width) * gain
            slope[b, at : at + 128, :] = gelu_slope(normed) * gain

    normed_slope(0)
    relay_cot(0)

    halo = [None] * batch
    for b in range(batch):
        for k in range(4):
            if k > 0:
                hid_in[k][b].wait_recv()
            if k == 2:
                hid_in[3][b] = push(hid.at[2, b], hid.at[3, b], {"chan": c1})
            w_rows = chan_rows(peers[k])

            @pl.when(has_hi)
            def _():
                term = dot_nn(hid[k, b], w_ref[0, w_rows, :])
                acc_hi[...] = term if k == 0 else acc_hi[...] + term

            @pl.when(has_lo)
            def _():
                term = dot_nn(hid[k, b], w_ref[2, w_rows, :])
                acc_lo[...] = term if k == 0 else acc_lo[...] + term

        to_hi = copy(y_hi.at[b], yr_lo.at[b], {"seq": up})
        to_lo = copy(y_lo.at[b], yr_hi.at[b], {"seq": down})
        halo[b] = (to_hi, to_lo)

        @pl.when(has_hi)
        def _():
            y_hi[b] = acc_hi[...].astype(BF16)
            to_hi.start()

        @pl.when(has_lo)
        def _():
            y_lo[b] = acc_lo[...].astype(BF16)
            to_lo.start()

        dil[b] = sum(dot_nn(hid[k, b], w_ref[1, chan_rows(peers[k]), :]) for k in range(4))

    def hidden_grad(b):
        cot_in[1][b].wait_recv()
        cot_in[3][b].wait_recv()
        hg[b] = sum(dot_nn(cot[j, b], wp_ref[j * width : (j + 1) * width, :]) for j in range(4))

    hidden_grad(0)
    for b in range(1, batch):
        normed_slope(b)
        relay_cot(b)

    back = [None] * batch
    for b in range(batch):
        to_hi, to_lo = halo[b]

        @pl.when(has_lo)
        def _():
            to_hi.wait_recv()
            dil[b] += yr_lo[b].astype(F32)

        @pl.when(has_hi)
        def _():
            to_lo.wait_recv()
            dil[b] += yr_hi[b].astype(F32)

        if b > 0:
            hidden_grad(b)
        value = dil[b]
        dg[b] = (hg[b] * gelu_slope(value)).astype(BF16)
        g_hi = copy(dg.at[b], dr_lo.at[b], {"seq": up})
        g_lo = copy(dg.at[b], dr_hi.at[b], {"seq": down})
        back[b] = (g_hi, g_lo)

        @pl.when(has_hi)
        def _():
            g_hi.start()

        @pl.when(has_lo)
        def _():
            g_lo.start()

        act[b] = gelu_value(value).astype(BF16)

    def point_grad(j):
        return sum(dot_tn(cot[j, b], act[b]) for b in range(batch))

    if scatter:
        qs[0] = point_grad(s1).astype(BF16)
        qs[1] = point_grad(s3).astype(BF16)
        q1 = push(qs, qr, {"seq": s1})

    first = [None] * batch
    cross = [None] * batch
    for b in range(batch):
        g_hi, g_lo = back[b]

        @pl.when(has_hi)
        def _():
            g_lo.wait_recv()

        @pl.when(has_lo)
        def _():
            g_hi.wait_recv()

        for k in (3, 1, 2, 0):
            w_rows = chan_rows(peers[k])
            part[...] = dot_nt(dg[b], w_ref[1, w_rows, :])

            @pl.when(has_hi)
            def _():
                part[...] += dot_nt(dr_hi[b], w_ref[0, w_rows, :])

            @pl.when(has_lo)
            def _():
                part[...] += dot_nt(dr_lo[b], w_ref[2, w_rows, :])

            if k == 3:
                ps[b, 1] = part[...].astype(BF16)
                cross[b] = push(ps.at[b, 1], pr.at[b, 1], {"chan": c1})
            elif k == 1:
                ps[b, 0] = part[...].astype(BF16)
                first[b] = push(ps.at[b, 0], pr.at[b, 0], {"chan": c1})
            elif k == 2:
                cross[b].wait_recv()
                xs[b] = (part[...] + pr[b, 1].astype(F32)).astype(BF16)
                cross[b] = push(xs.at[b], xr.at[b], {"chan": c2})
            else:
                sg[b] = part[...]

    if scatter:
        q1.wait_recv()
        qs2[...] = (point_grad(s2) + qr[1].astype(F32)).astype(BF16)
        q2 = push(qs2, qr2, {"seq": s2})
        pg_ref[...] = point_grad(s) + qr[0].astype(F32)
    else:
        for j in range(4):
            pg_ref[j * width : (j + 1) * width, :] = point_grad(j)

    inner = [None] * batch
    for b in range(batch):
        first[b].wait_recv()
        cross[b].wait_recv()
        for at in range(0, rows, 128):
            here = slice(at, at + 128)
            raw = sg[b, here, :] + pr[b, 0, here, :].astype(F32) + xr[b, here, :].astype(F32)
            scaled = raw * slope[b, here, :]
            sg[b, here, :] = scaled
            unit = x_ref[b, here, :].astype(F32) * widen(rs[b, here, :], width)
            pn[b, 0, :, here] = jnp.broadcast_to(lanes_to_row(scaled * unit), (8, 128))
        inner[b] = [push(pn.at[b, 0], pn.at[b, k], {"chan": peers[k]}) for k in (2, 3, 1)]
    if scatter:
        q2.wait_recv()
        pg_ref[...] += qr2[...].astype(F32)
    for b in range(batch):
        for handle in inner[b]:
            handle.wait_recv()
        for at in range(0, rows, 128):
            here = slice(at, at + 128)
            total = pn[b, 0, 0:1, here] + pn[b, 1, 0:1, here] + pn[b, 2, 0:1, here] + pn[b, 3, 0:1, here]
            mean = widen(row_to_columns(total * (1.0 / channels)), width)
            scale = widen(rs[b, here, :], width)
            unit = x_ref[b, here, :].astype(F32) * scale
            out_ref[b, here, :] = (
                ct_ref[b, here, :].astype(F32) + scale * (sg[b, here, :] - unit * mean)
            ).astype(BF16)

    for handle in sent:
        handle.wait_send()
    for b in range(batch):
        for hi, lo in (halo[b], back[b]):

            @pl.when(has_hi)
            def _():
                hi.wait_send()

            @pl.when(has_lo)
            def _():
                lo.wait_send()


def per_device(seq_n, inputs, cotangent, dilated_weight, w_point, norm_gain):
    batch, rows, width = inputs.shape
    channels = norm_gain.shape[0]
    units = w_point.shape[1]
    scatter = seq_n * width == channels
    wide = lambda *lead: pltpu.VMEM((*lead, rows, width), BF16)
    thin = lambda *lead: pltpu.VMEM((*lead, rows, units), BF16)
    thin32 = lambda *lead: pltpu.VMEM((*lead, rows, units), F32)
    pg_rows = width if scatter else channels
    block = lambda *lead: pltpu.VMEM((*lead, width, units), BF16)
    vmem = pl.BlockSpec(memory_space=pltpu.VMEM)
    input_grad, point_grad = pl.pallas_call(
        functools.partial(kernel, seq_n, DILATION_STEP // rows, scatter),
        out_shape=(
            jax.ShapeDtypeStruct(inputs.shape, BF16),
            jax.ShapeDtypeStruct((pg_rows, units), F32),
        ),
        in_specs=[vmem] * 5,
        out_specs=(vmem, vmem),
        scratch_shapes=[
            wide(4, batch),
            wide(4, batch),
            pltpu.VMEM((4, 8, batch * rows), F32),
            pltpu.VMEM((batch, rows, 128), F32),
            pltpu.VMEM((batch, rows, width), F32),
            thin32(batch),
            thin32(),
            thin32(),
            thin(batch),
            thin32(batch),
            thin(batch), thin(batch), thin(batch), thin(batch),
            thin(batch), thin(batch), thin(batch),
            pltpu.VMEM((rows, width), F32),
            wide(batch, 2), wide(batch, 2),
            wide(batch), wide(batch),
            pltpu.VMEM((batch, rows, width), F32),
            pltpu.VMEM((batch, 4, 8, rows), F32),
            block(2), block(2), block(), block(),
            pltpu.SemaphoreType.DMA((N_SEMS,)),
            pltpu.SemaphoreType.DMA((N_SEMS,)),
        ],
        compiler_params=pltpu.CompilerParams(
            collective_id=0, has_side_effects=True, vmem_limit_bytes=40 * 1024 * 1024
        ),
    )(inputs, cotangent, dilated_weight, w_point, norm_gain.reshape(1, channels))
    if not scatter:
        point_grad = lax.psum_scatter(point_grad, "seq", scatter_dimension=0, tiled=True)
    return (input_grad, point_grad)


def solution(mesh):
    placed = (
        P("grp", "seq", "chan"),
        P("grp", "seq", "chan"),
        P(None, None, "chan"),
        P(None, "chan"),
        P(),
    )
    return jax.shard_map(
        functools.partial(per_device, mesh.shape["seq"]),
        mesh=mesh,
        in_specs=placed,
        out_specs=(P("grp", "seq", "chan"), P(("grp", "seq"), "chan")),
        check_vma=False,
    )
```

```python
import functools
import math

import jax
import jax.numpy as jnp
from jax import lax
from jax.experimental import pallas as pl
from jax.experimental.pallas import tpu as pltpu
from jax.sharding import PartitionSpec as P

DILATION_STEP = 512
epsilon = 1e-05
N_SEMS = 64
F32 = jnp.float32
BF16 = jnp.bfloat16
MESH = pl.DeviceIdType.MESH


def gelu_value(values):
    return 0.5 * values * (1.0 + lax.erf(values * (1.0 / math.sqrt(2.0))))


def gelu_slope(values):
    return 0.5 * (1.0 + lax.erf(values * (1.0 / math.sqrt(2.0)))) + values * jnp.exp(
        -0.5 * values * values
    ) * (1.0 / math.sqrt(2.0 * math.pi))


def dot_nn(a, b):
    return lax.dot_general(a, b, (((1,), (0,)), ((), ())), preferred_element_type=F32)


def dot_nt(a, b):
    return lax.dot_general(a, b, (((1,), (1,)), ((), ())), preferred_element_type=F32)


def dot_tn(a, b):
    return lax.dot_general(a, b, (((0,), (0,)), ((), ())), preferred_element_type=F32)


def lanes_to_row(values):
    total = values[:, 0:128]
    for at in range(128, values.shape[1], 128):
        total = total + values[:, at : at + 128]
    return jnp.sum(total.T, axis=0, keepdims=True)


def row_to_columns(row):
    return jnp.broadcast_to(row, (128, 128)).T


def widen(columns, width):
    return jnp.concatenate([columns] * (width // 128), axis=1)


def kernel(
    seq_n, stride, scatter, x_hbm, ct_hbm, w_hbm, wp_hbm, gain_ref, out_ref, pg_ref, qr2,
    x_ref, w_ref, wp_ref,
    hid, cot, ss, rs, slope, dil, acc_lo, acc_hi, act, hg, y_lo, y_hi, yr_lo, yr_hi, dg, dr_lo, dr_hi,
    part, ps, pr, xf, xs, xr, sg, pn, qs, qr, qs2, send_sem, recv_sem, load_sem,
):
    batch, rows, width = x_ref.shape
    channels = gain_ref.shape[1]
    c = lax.axis_index("chan")
    s = lax.axis_index("seq")
    c1 = c + 1 - 2 * lax.rem(c, 2)
    c2 = lax.rem(c + 2, 4)
    c3 = 3 - c
    peers = (c, c1, c2, c3)
    s1 = s + 1 - 2 * lax.rem(s, 2)
    s2 = lax.rem(s + 2, 4)
    s3 = 3 - s
    has_hi = s + stride < seq_n
    has_lo = s >= stride
    up = lax.rem(s + stride, seq_n)
    down = lax.rem(s - stride + seq_n, seq_n)

    count = [0]
    sent = []

    def copy(src, dst, device):
        k = count[0]
        count[0] += 1
        return pltpu.make_async_remote_copy(
            src_ref=src, dst_ref=dst, send_sem=send_sem.at[k], recv_sem=recv_sem.at[k],
            device_id=device, device_id_type=MESH,
        )

    def push(src, dst, device):
        handle = copy(src, dst, device)
        handle.start()
        sent.append(handle)
        return handle

    def chan_rows(ch):
        return pl.ds(pl.multiple_of(ch * width, width), width)

    loads = [
        pltpu.make_async_copy(src, dst, load_sem.at[i])
        for i, (src, dst) in enumerate(
            ((x_hbm, x_ref), (ct_hbm, cot.at[c]), (w_hbm, w_ref), (wp_hbm, wp_ref))
        )
    ]
    for load in loads:
        load.start()

    barrier = pltpu.get_barrier_semaphore()
    for peer in (c1, c2, c3):
        pl.semaphore_signal(barrier, inc=1, device_id={"chan": peer}, device_id_type=MESH)

    @pl.when(has_hi)
    def _():
        pl.semaphore_signal(barrier, inc=1, device_id={"seq": up}, device_id_type=MESH)

    @pl.when(has_lo)
    def _():
        pl.semaphore_signal(barrier, inc=1, device_id={"seq": down}, device_id_type=MESH)

    if scatter:
        pl.semaphore_signal(barrier, inc=1, device_id={"seq": s1}, device_id_type=MESH)

    loads[0].wait()
    for b in range(batch):
        for at in range(0, rows, 128):
            v = x_ref[b, at : at + 128, :].astype(F32)
            ss[0, :, b * rows + at : b * rows + at + 128] = jnp.broadcast_to(lanes_to_row(v * v), (8, 128))

    loads[1].wait()
    ways = has_hi.astype(jnp.int32) + has_lo.astype(jnp.int32)
    pl.semaphore_wait(barrier, ways + (4 if scatter else 3))

    ss_in = [push(ss.at[0], ss.at[k], {"chan": peers[k]}) for k in (2, 3, 1)]
    cot_in = [[None] * batch for _ in range(4)]
    hid_in = [[None] * batch for _ in range(4)]

    def spread_cot(b):
        cot_in[2][b] = push(cot.at[c, b], cot.at[c, b], {"chan": c2})
        cot_in[1][b] = push(cot.at[c, b], cot.at[c, b], {"chan": c1})

    def relay_cot(b):
        copy_in = cot_in[2][b]
        copy_in.wait_recv()
        cot_in[3][b] = push(cot.at[c2, b], cot.at[c2, b], {"chan": c1})

    spread_cot(0)
    for handle in ss_in:
        handle.wait_recv()
    gain = gain_ref[:, chan_rows(c)]
    for b in range(batch):
        for at in range(0, rows, 128):
            here = slice(b * rows + at, b * rows + at + 128)
            total = ss[0, 0:1, here] + ss[1, 0:1, here] + ss[2, 0:1, here] + ss[3, 0:1, here]
            columns = row_to_columns(lax.rsqrt(total * (1.0 / channels) + epsilon))
            rs[b, at : at + 128, :] = columns
            normed = x_ref[b, at : at + 128, :].astype(F32) * widen(columns, width) * gain
            hid[0, b, at : at + 128, :] = gelu_value(normed).astype(BF16)
        hid_in[2][b] = push(hid.at[0, b], hid.at[2, b], {"chan": c2})
        hid_in[1][b] = push(hid.at[0, b], hid.at[1, b], {"chan": c1})
    for b in range(1, batch):
        spread_cot(b)

    def normed_slope(b):
        for at in range(0, rows, 128):
            normed = x_ref[b, at : at + 128, :].astype(F32) * widen(rs[b, at : at + 128, :], width) * gain
            slope[b, at : at + 128, :] = gelu_slope(normed) * gain

    normed_slope(0)
    relay_cot(0)

    loads[2].wait()
    loads[3].wait()
    halo = [None] * batch
    for b in range(batch):
        for k in range(4):
            if k > 0:
                hid_in[k][b].wait_recv()
            if k == 2:
                hid_in[3][b] = push(hid.at[2, b], hid.at[3, b], {"chan": c1})
            w_rows = chan_rows(peers[k])

            @pl.when(has_hi)
            def _():
                term = dot_nt(w_ref[0, :, w_rows], hid[k, b])
                acc_hi[...] = term if k == 0 else acc_hi[...] + term

            @pl.when(has_lo)
            def _():
                term = dot_nt(w_ref[2, :, w_rows], hid[k, b])
                acc_lo[...] = term if k == 0 else acc_lo[...] + term

        to_hi = copy(y_hi.at[b], yr_lo.at[b], {"seq": up})
        to_lo = copy(y_lo.at[b], yr_hi.at[b], {"seq": down})
        halo[b] = (to_hi, to_lo)

        @pl.when(has_hi)
        def _():
            y_hi[b] = acc_hi[...].astype(BF16)
            to_hi.start()

        @pl.when(has_lo)
        def _():
            y_lo[b] = acc_lo[...].astype(BF16)
            to_lo.start()

        dil[b] = sum(dot_nt(w_ref[1, :, chan_rows(peers[k])], hid[k, b]) for k in range(4))

    def hidden_grad(b):
        cot_in[1][b].wait_recv()
        cot_in[3][b].wait_recv()
        hg[b] = sum(dot_nt(wp_ref[:, j * width : (j + 1) * width], cot[j, b]) for j in range(4))

    hidden_grad(0)
    for b in range(1, batch):
        normed_slope(b)
        relay_cot(b)

    back = [None] * batch
    for b in range(batch):
        to_hi, to_lo = halo[b]

        @pl.when(has_lo)
        def _():
            to_hi.wait_recv()
            dil[b] += yr_lo[b].astype(F32)

        @pl.when(has_hi)
        def _():
            to_lo.wait_recv()
            dil[b] += yr_hi[b].astype(F32)

        if b > 0:
            hidden_grad(b)
        value = dil[b]
        dg[b] = (hg[b] * gelu_slope(value)).astype(BF16)
        g_hi = copy(dg.at[b], dr_lo.at[b], {"seq": up})
        g_lo = copy(dg.at[b], dr_hi.at[b], {"seq": down})
        back[b] = (g_hi, g_lo)

        @pl.when(has_hi)
        def _():
            g_hi.start()

        @pl.when(has_lo)
        def _():
            g_lo.start()

        act[b] = gelu_value(value).astype(BF16)

    def point_grad(j):
        return sum(dot_nn(act[b], cot[j, b]) for b in range(batch))

    first = [None] * batch
    cross = [None] * batch

    def partial_grads(b):
        g_hi, g_lo = back[b]

        @pl.when(has_hi)
        def _():
            g_lo.wait_recv()

        @pl.when(has_lo)
        def _():
            g_hi.wait_recv()

        part[...] = dot_tn(dg[b], w_ref[1])

        @pl.when(has_hi)
        def _():
            part[...] += dot_tn(dr_hi[b], w_ref[0])

        @pl.when(has_lo)
        def _():
            part[...] += dot_tn(dr_lo[b], w_ref[2])

        ps[b, 1] = part[:, chan_rows(c3)].astype(BF16)
        cross[b] = push(ps.at[b, 1], pr.at[b, 1], {"chan": c1})
        ps[b, 0] = part[:, chan_rows(c1)].astype(BF16)
        first[b] = push(ps.at[b, 0], pr.at[b, 0], {"chan": c1})
        sg[b] = part[:, chan_rows(c)]
        xf[b] = part[:, chan_rows(c2)]

    def cross_over(b):
        cross[b].wait_recv()
        xs[b] = (xf[b] + pr[b, 1].astype(F32)).astype(BF16)
        cross[b] = push(xs.at[b], xr.at[b], {"chan": c2})

    partial_grads(0)
    if scatter:
        qs[0] = point_grad(s1).astype(BF16)
        qs[1] = point_grad(s3).astype(BF16)
        q1 = push(qs, qr, {"seq": s1})
    cross_over(0)
    for b in range(1, batch):
        partial_grads(b)
        if scatter and b == 1:
            pg_ref[...] = point_grad(s)
        cross_over(b)
    if scatter:
        q1.wait_recv()
        qs2[...] = (point_grad(s2) + qr[1].astype(F32)).astype(BF16)
        q2 = push(qs2, qr2, {"seq": s2})
        pg_ref[...] += qr[0].astype(F32)
    else:
        for j in range(4):
            pg_ref[:, j * width : (j + 1) * width] = point_grad(j)
        qr2[...] = jnp.zeros(qr2.shape, BF16)

    inner = [None] * batch
    for b in range(batch):
        first[b].wait_recv()
        cross[b].wait_recv()
        for at in range(0, rows, 128):
            here = slice(at, at + 128)
            raw = sg[b, here, :] + pr[b, 0, here, :].astype(F32) + xr[b, here, :].astype(F32)
            scaled = raw * slope[b, here, :]
            sg[b, here, :] = scaled
            unit = x_ref[b, here, :].astype(F32) * widen(rs[b, here, :], width)
            pn[b, 0, :, here] = jnp.broadcast_to(lanes_to_row(scaled * unit), (8, 128))
        inner[b] = [push(pn.at[b, 0], pn.at[b, k], {"chan": peers[k]}) for k in (2, 3, 1)]
    if scatter:
        q2.wait_recv()
    for b in range(batch):
        for handle in inner[b]:
            handle.wait_recv()
        for at in range(0, rows, 128):
            here = slice(at, at + 128)
            total = pn[b, 0, 0:1, here] + pn[b, 1, 0:1, here] + pn[b, 2, 0:1, here] + pn[b, 3, 0:1, here]
            mean = widen(row_to_columns(total * (1.0 / channels)), width)
            scale = widen(rs[b, here, :], width)
            unit = x_ref[b, here, :].astype(F32) * scale
            out_ref[b, here, :] = scale * (sg[b, here, :] - unit * mean)

    for handle in sent:
        handle.wait_send()
    for b in range(batch):
        for hi, lo in (halo[b], back[b]):

            @pl.when(has_hi)
            def _():
                hi.wait_send()

            @pl.when(has_lo)
            def _():
                lo.wait_send()


def per_device(seq_n, inputs, cotangent, dilated_weight, w_point, norm_gain):
    batch, rows, width = inputs.shape
    channels = norm_gain.shape[0]
    units = w_point.shape[1]
    scatter = seq_n * width == channels
    wide = lambda *lead: pltpu.VMEM((*lead, rows, width), BF16)
    thin = lambda *lead: pltpu.VMEM((*lead, units, rows), BF16)
    thin32 = lambda *lead: pltpu.VMEM((*lead, units, rows), F32)
    pg_rows = width if scatter else channels
    block = lambda *lead: pltpu.VMEM((*lead, units, width), BF16)
    vmem = pl.BlockSpec(memory_space=pltpu.VMEM)
    hbm = pl.BlockSpec(memory_space=pltpu.HBM)
    branch_grad, point_grad, point_rest = pl.pallas_call(
        functools.partial(kernel, seq_n, DILATION_STEP // rows, scatter),
        out_shape=(
            jax.ShapeDtypeStruct(inputs.shape, F32),
            jax.ShapeDtypeStruct((units, pg_rows), F32),
            jax.ShapeDtypeStruct((units, width), BF16),
        ),
        in_specs=[hbm] * 4 + [vmem],
        out_specs=(vmem, vmem, vmem),
        scratch_shapes=[
            wide(batch),
            pltpu.VMEM((3, units, channels), BF16),
            pltpu.VMEM((units, channels), BF16),
            wide(4, batch),
            wide(4, batch),
            pltpu.VMEM((4, 8, batch * rows), F32),
            pltpu.VMEM((batch, rows, 128), F32),
            pltpu.VMEM((batch, rows, width), F32),
            thin32(batch),
            thin32(),
            thin32(),
            thin(batch),
            thin32(batch),
            thin(batch), thin(batch), thin(batch), thin(batch),
            thin(batch), thin(batch), thin(batch),
            pltpu.VMEM((rows, channels), F32),
            wide(batch, 2), wide(batch, 2),
            pltpu.VMEM((batch, rows, width), F32),
            wide(batch), wide(batch),
            pltpu.VMEM((batch, rows, width), F32),
            pltpu.VMEM((batch, 4, 8, rows), F32),
            block(2), block(2), block(),
            pltpu.SemaphoreType.DMA((N_SEMS,)),
            pltpu.SemaphoreType.DMA((N_SEMS,)),
            pltpu.SemaphoreType.DMA((4,)),
        ],
        compiler_params=pltpu.CompilerParams(
            collective_id=0, has_side_effects=True, vmem_limit_bytes=61 * 1024 * 1024
        ),
    )(
        inputs, cotangent, dilated_weight.transpose(0, 2, 1), w_point.T, norm_gain.reshape(1, channels)
    )
    input_grad = (cotangent.astype(F32) + branch_grad).astype(BF16)
    if scatter:
        point_grad = (point_grad + point_rest.astype(F32)).T
    else:
        point_grad = point_grad.T
        point_grad = lax.psum_scatter(point_grad, "seq", scatter_dimension=0, tiled=True)
    return (input_grad, point_grad)


def solution(mesh):
    placed = (
        P("grp", "seq", "chan"),
        P("grp", "seq", "chan"),
        P(None, None, "chan"),
        P(None, "chan"),
        P(),
    )
    return jax.shard_map(
        functools.partial(per_device, mesh.shape["seq"]),
        mesh=mesh,
        in_specs=placed,
        out_specs=(P("grp", "seq", "chan"), P(("grp", "seq"), "chan")),
        check_vma=False,
    )
```

```python
import functools
import math

import jax
import jax.numpy as jnp
from jax import lax
from jax.experimental import pallas as pl
from jax.experimental.pallas import tpu as pltpu
from jax.sharding import PartitionSpec as P

DILATION_STEP = 512
epsilon = 1e-05
N_SEMS = 96
F32 = jnp.float32
BF16 = jnp.bfloat16
MESH = pl.DeviceIdType.MESH


def gelu_value(values):
    return 0.5 * values * (1.0 + lax.erf(values * (1.0 / math.sqrt(2.0))))


def gelu_slope(values):
    return 0.5 * (1.0 + lax.erf(values * (1.0 / math.sqrt(2.0)))) + values * jnp.exp(
        -0.5 * values * values
    ) * (1.0 / math.sqrt(2.0 * math.pi))


def dot_nn(a, b):
    return lax.dot_general(a, b, (((1,), (0,)), ((), ())), preferred_element_type=F32)


def dot_nt(a, b):
    return lax.dot_general(a, b, (((1,), (1,)), ((), ())), preferred_element_type=F32)


def dot_tn(a, b):
    return lax.dot_general(a, b, (((0,), (0,)), ((), ())), preferred_element_type=F32)


def lanes_to_row(values):
    total = values[:, 0:128]
    for at in range(128, values.shape[1], 128):
        total = total + values[:, at : at + 128]
    return jnp.sum(total.T, axis=0, keepdims=True)


def row_to_columns(row):
    return jnp.broadcast_to(row, (128, 128)).T


def widen(columns, width):
    return jnp.concatenate([columns] * (width // 128), axis=1)


def kernel(
    seq_n, stride, scatter, x_hbm, ct_hbm, w_hbm, wp_hbm, gain_ref, out_ref, pg_ref, qr2,
    x_ref, w_ref, wp_ref,
    hid, cot, ss, rs, slope, dil, acc_lo, acc_hi, act, hg, y_lo, y_hi, yr_lo, yr_hi, dg, dr_lo, dr_hi,
    part, ps, pr, xf, xs, xr, sg, pn, qs, qr, qs2, send_sem, recv_sem, load_sem,
):
    batch, rows, width = x_ref.shape
    channels = gain_ref.shape[1]
    c = lax.axis_index("chan")
    s = lax.axis_index("seq")
    c1 = c + 1 - 2 * lax.rem(c, 2)
    c2 = lax.rem(c + 2, 4)
    c3 = 3 - c
    peers = (c, c1, c2, c3)
    s1 = s + 1 - 2 * lax.rem(s, 2)
    s2 = lax.rem(s + 2, 4)
    s3 = 3 - s
    has_hi = s + stride < seq_n
    has_lo = s >= stride
    up = lax.rem(s + stride, seq_n)
    down = lax.rem(s - stride + seq_n, seq_n)

    count = [0]
    sent = []

    def copy(src, dst, device):
        k = count[0]
        count[0] += 1
        return pltpu.make_async_remote_copy(
            src_ref=src, dst_ref=dst, send_sem=send_sem.at[k], recv_sem=recv_sem.at[k],
            device_id=device, device_id_type=MESH,
        )

    def push(src, dst, device):
        handle = copy(src, dst, device)
        handle.start()
        sent.append(handle)
        return handle

    def chan_rows(ch):
        return pl.ds(pl.multiple_of(ch * width, width), width)

    loads = [
        pltpu.make_async_copy(src, dst, load_sem.at[i])
        for i, (src, dst) in enumerate(
            ((x_hbm, x_ref), (ct_hbm, cot.at[c]), (w_hbm, w_ref), (wp_hbm, wp_ref))
        )
    ]
    for load in loads:
        load.start()

    barrier = pltpu.get_barrier_semaphore()
    for peer in (c1, c2, c3):
        pl.semaphore_signal(barrier, inc=1, device_id={"chan": peer}, device_id_type=MESH)

    @pl.when(has_hi)
    def _():
        pl.semaphore_signal(barrier, inc=1, device_id={"seq": up}, device_id_type=MESH)

    @pl.when(has_lo)
    def _():
        pl.semaphore_signal(barrier, inc=1, device_id={"seq": down}, device_id_type=MESH)

    if scatter:
        pl.semaphore_signal(barrier, inc=1, device_id={"seq": s1}, device_id_type=MESH)

    loads[0].wait()
    for b in range(batch):
        for at in range(0, rows, 128):
            v = x_ref[b, at : at + 128, :].astype(F32)
            ss[0, :, b * rows + at : b * rows + at + 128] = jnp.broadcast_to(lanes_to_row(v * v), (8, 128))

    loads[1].wait()
    ways = has_hi.astype(jnp.int32) + has_lo.astype(jnp.int32)
    pl.semaphore_wait(barrier, ways + (4 if scatter else 3))

    ss_in = [push(ss.at[0], ss.at[k], {"chan": peers[k]}) for k in (2, 3, 1)]
    cot_in = [[None] * batch for _ in range(4)]
    hid_in = [[None] * batch for _ in range(4)]

    def spread_cot(b):
        cot_in[2][b] = push(cot.at[c, b], cot.at[c, b], {"chan": c2})
        cot_in[1][b] = push(cot.at[c, b], cot.at[c, b], {"chan": c1})

    def relay_cot(b):
        copy_in = cot_in[2][b]
        copy_in.wait_recv()
        cot_in[3][b] = push(cot.at[c2, b], cot.at[c2, b], {"chan": c1})

    spread_cot(0)
    for handle in ss_in:
        handle.wait_recv()
    gain = gain_ref[:, chan_rows(c)]
    for b in range(batch):
        for at in range(0, rows, 128):
            here = slice(b * rows + at, b * rows + at + 128)
            total = ss[0, 0:1, here] + ss[1, 0:1, here] + ss[2, 0:1, here] + ss[3, 0:1, here]
            columns = row_to_columns(lax.rsqrt(total * (1.0 / channels) + epsilon))
            rs[b, at : at + 128, :] = columns
            normed = x_ref[b, at : at + 128, :].astype(F32) * widen(columns, width) * gain
            hid[0, b, at : at + 128, :] = gelu_value(normed).astype(BF16)
        hid_in[2][b] = push(hid.at[0, b], hid.at[2, b], {"chan": c2})
        hid_in[1][b] = push(hid.at[0, b], hid.at[1, b], {"chan": c1})
    for b in range(1, batch):
        spread_cot(b)

    def normed_slope(b):
        for at in range(0, rows, 128):
            normed = x_ref[b, at : at + 128, :].astype(F32) * widen(rs[b, at : at + 128, :], width) * gain
            slope[b, at : at + 128, :] = gelu_slope(normed) * gain

    normed_slope(0)
    relay_cot(0)

    loads[2].wait()
    loads[3].wait()
    halo = [None] * batch
    for b in range(batch):
        for k in range(4):
            if k > 0:
                hid_in[k][b].wait_recv()
            if k == 2:
                hid_in[3][b] = push(hid.at[2, b], hid.at[3, b], {"chan": c1})
            w_rows = chan_rows(peers[k])

            @pl.when(has_hi)
            def _():
                term = dot_nt(w_ref[0, :, w_rows], hid[k, b])
                acc_hi[...] = term if k == 0 else acc_hi[...] + term

            @pl.when(has_lo)
            def _():
                term = dot_nt(w_ref[2, :, w_rows], hid[k, b])
                acc_lo[...] = term if k == 0 else acc_lo[...] + term

        to_hi = copy(y_hi.at[b], yr_lo.at[b], {"seq": up})
        to_lo = copy(y_lo.at[b], yr_hi.at[b], {"seq": down})
        halo[b] = (to_hi, to_lo)

        @pl.when(has_hi)
        def _():
            y_hi[b] = acc_hi[...].astype(BF16)
            to_hi.start()

        @pl.when(has_lo)
        def _():
            y_lo[b] = acc_lo[...].astype(BF16)
            to_lo.start()

        dil[b] = sum(dot_nt(w_ref[1, :, chan_rows(peers[k])], hid[k, b]) for k in range(4))

    def hidden_grad(b):
        cot_in[1][b].wait_recv()
        cot_in[3][b].wait_recv()
        hg[b] = sum(dot_nt(wp_ref[:, j * width : (j + 1) * width], cot[j, b]) for j in range(4))

    hidden_grad(0)
    for b in range(1, batch):
        normed_slope(b)
        relay_cot(b)

    back = [None] * batch
    for b in range(batch):
        to_hi, to_lo = halo[b]

        @pl.when(has_lo)
        def _():
            to_hi.wait_recv()
            dil[b] += yr_lo[b].astype(F32)

        @pl.when(has_hi)
        def _():
            to_lo.wait_recv()
            dil[b] += yr_hi[b].astype(F32)

        if b > 0:
            hidden_grad(b)
        value = dil[b]
        dg[b] = (hg[b] * gelu_slope(value)).astype(BF16)
        g_hi = copy(dg.at[b], dr_lo.at[b], {"seq": up})
        g_lo = copy(dg.at[b], dr_hi.at[b], {"seq": down})
        back[b] = (g_hi, g_lo)

        @pl.when(has_hi)
        def _():
            g_hi.start()

        @pl.when(has_lo)
        def _():
            g_lo.start()

        act[b] = gelu_value(value).astype(BF16)

    def point_grad(j):
        return sum(dot_nn(act[b], cot[j, b]) for b in range(batch))

    first = [None] * batch
    cross = [None] * batch

    def partial_grads(b):
        g_hi, g_lo = back[b]

        @pl.when(has_hi)
        def _():
            g_lo.wait_recv()

        @pl.when(has_lo)
        def _():
            g_hi.wait_recv()

        part[...] = dot_tn(dg[b], w_ref[1])

        @pl.when(has_hi)
        def _():
            part[...] += dot_tn(dr_hi[b], w_ref[0])

        @pl.when(has_lo)
        def _():
            part[...] += dot_tn(dr_lo[b], w_ref[2])

        ps[b, 1] = part[:, chan_rows(c3)].astype(BF16)
        cross[b] = push(ps.at[b, 1], pr.at[b, 1], {"chan": c1})
        ps[b, 0] = part[:, chan_rows(c1)].astype(BF16)
        first[b] = push(ps.at[b, 0], pr.at[b, 0], {"chan": c1})
        sg[b] = part[:, chan_rows(c)]
        xf[b] = part[:, chan_rows(c2)]

    def cross_over(b):
        cross[b].wait_recv()
        xs[b] = (xf[b] + pr[b, 1].astype(F32)).astype(BF16)
        cross[b] = push(xs.at[b], xr.at[b], {"chan": c2})

    partial_grads(0)
    if scatter:
        qs[0] = point_grad(s1).astype(BF16)
        qs[1] = point_grad(s3).astype(BF16)
        q1 = push(qs, qr, {"seq": s1})
    cross_over(0)
    for b in range(1, batch):
        partial_grads(b)
        if scatter and b == 1:
            pg_ref[...] = point_grad(s)
        cross_over(b)
    if scatter:
        q1.wait_recv()
        qs2[...] = (point_grad(s2) + qr[1].astype(F32)).astype(BF16)
        q2 = push(qs2, qr2, {"seq": s2})
        pg_ref[...] += qr[0].astype(F32)
    else:
        for j in range(4):
            pg_ref[:, j * width : (j + 1) * width] = point_grad(j)
        qr2[...] = jnp.zeros(qr2.shape, BF16)

    inner = [None] * batch
    for b in range(batch):
        first[b].wait_recv()
        cross[b].wait_recv()
        for at in range(0, rows, 128):
            here = slice(at, at + 128)
            raw = sg[b, here, :] + pr[b, 0, here, :].astype(F32) + xr[b, here, :].astype(F32)
            scaled = raw * slope[b, here, :]
            sg[b, here, :] = scaled
            unit = x_ref[b, here, :].astype(F32) * widen(rs[b, here, :], width)
            pn[b, 0, :, here] = jnp.broadcast_to(lanes_to_row(scaled * unit), (8, 128))
        inner[b] = [push(pn.at[b, 0], pn.at[b, k], {"chan": peers[k]}) for k in (2, 3, 1)]
    if scatter:
        q2.wait_recv()
    for b in range(batch):
        for handle in inner[b]:
            handle.wait_recv()
        for at in range(0, rows, 128):
            here = slice(at, at + 128)
            total = pn[b, 0, 0:1, here] + pn[b, 1, 0:1, here] + pn[b, 2, 0:1, here] + pn[b, 3, 0:1, here]
            mean = widen(row_to_columns(total * (1.0 / channels)), width)
            scale = widen(rs[b, here, :], width)
            unit = x_ref[b, here, :].astype(F32) * scale
            out_ref[b, here, :] = scale * (sg[b, here, :] - unit * mean)

    for handle in sent:
        handle.wait_send()
    for b in range(batch):
        for hi, lo in (halo[b], back[b]):

            @pl.when(has_hi)
            def _():
                hi.wait_send()

            @pl.when(has_lo)
            def _():
                lo.wait_send()


def per_device(seq_n, inputs, cotangent, dilated_weight, w_point, norm_gain):
    stride = DILATION_STEP // inputs.shape[1]
    rows, width = 128, inputs.shape[2]
    batch = inputs.shape[0] * inputs.shape[1] // rows
    cut = (batch, rows, width)
    channels = norm_gain.shape[0]
    units = w_point.shape[1]
    scatter = seq_n * width == channels
    wide = lambda *lead: pltpu.VMEM((*lead, rows, width), BF16)
    thin = lambda *lead: pltpu.VMEM((*lead, units, rows), BF16)
    thin32 = lambda *lead: pltpu.VMEM((*lead, units, rows), F32)
    pg_rows = width if scatter else channels
    block = lambda *lead: pltpu.VMEM((*lead, units, width), BF16)
    vmem = pl.BlockSpec(memory_space=pltpu.VMEM)
    hbm = pl.BlockSpec(memory_space=pltpu.HBM)
    branch_grad, point_grad, point_rest = pl.pallas_call(
        functools.partial(kernel, seq_n, stride, scatter),
        out_shape=(
            jax.ShapeDtypeStruct(cut, F32),
            jax.ShapeDtypeStruct((units, pg_rows), F32),
            jax.ShapeDtypeStruct((units, width), BF16),
        ),
        in_specs=[hbm] * 4 + [vmem],
        out_specs=(vmem, vmem, vmem),
        scratch_shapes=[
            wide(batch),
            pltpu.VMEM((3, units, channels), BF16),
            pltpu.VMEM((units, channels), BF16),
            wide(4, batch),
            wide(4, batch),
            pltpu.VMEM((4, 8, batch * rows), F32),
            pltpu.VMEM((batch, rows, 128), F32),
            pltpu.VMEM((batch, rows, width), F32),
            thin32(batch),
            thin32(),
            thin32(),
            thin(batch),
            thin32(batch),
            thin(batch), thin(batch), thin(batch), thin(batch),
            thin(batch), thin(batch), thin(batch),
            pltpu.VMEM((rows, channels), F32),
            wide(batch, 2), wide(batch, 2),
            pltpu.VMEM((batch, rows, width), F32),
            wide(batch), wide(batch),
            pltpu.VMEM((batch, rows, width), F32),
            pltpu.VMEM((batch, 4, 8, rows), F32),
            block(2), block(2), block(),
            pltpu.SemaphoreType.DMA((N_SEMS,)),
            pltpu.SemaphoreType.DMA((N_SEMS,)),
            pltpu.SemaphoreType.DMA((4,)),
        ],
        compiler_params=pltpu.CompilerParams(
            collective_id=0, has_side_effects=True, vmem_limit_bytes=61 * 1024 * 1024
        ),
    )(
        inputs.reshape(cut), cotangent.reshape(cut), dilated_weight.transpose(0, 2, 1), w_point.T, norm_gain.reshape(1, channels)
    )
    input_grad = (cotangent.astype(F32) + branch_grad.reshape(cotangent.shape)).astype(BF16)
    if scatter:
        point_grad = (point_grad + point_rest.astype(F32)).T
    else:
        point_grad = point_grad.T
        point_grad = lax.psum_scatter(point_grad, "seq", scatter_dimension=0, tiled=True)
    return (input_grad, point_grad)


def solution(mesh):
    placed = (
        P("grp", "seq", "chan"),
        P("grp", "seq", "chan"),
        P(None, None, "chan"),
        P(None, "chan"),
        P(),
    )
    return jax.shard_map(
        functools.partial(per_device, mesh.shape["seq"]),
        mesh=mesh,
        in_specs=placed,
        out_specs=(P("grp", "seq", "chan"), P(("grp", "seq"), "chan")),
        check_vma=False,
    )
```

```python
import functools
import math

import jax
import jax.numpy as jnp
from jax import lax
from jax.experimental import pallas as pl
from jax.experimental.pallas import tpu as pltpu
from jax.sharding import PartitionSpec as P

DILATION_STEP = 512
epsilon = 1e-05
N_SEMS = 96
F32 = jnp.float32
BF16 = jnp.bfloat16
MESH = pl.DeviceIdType.MESH


def gelu_value(values):
    return 0.5 * values * (1.0 + lax.erf(values * (1.0 / math.sqrt(2.0))))


def gelu_slope(values):
    return 0.5 * (1.0 + lax.erf(values * (1.0 / math.sqrt(2.0)))) + values * jnp.exp(
        -0.5 * values * values
    ) * (1.0 / math.sqrt(2.0 * math.pi))


def dot_nn(a, b):
    return lax.dot_general(a, b, (((1,), (0,)), ((), ())), preferred_element_type=F32)


def dot_nt(a, b):
    return lax.dot_general(a, b, (((1,), (1,)), ((), ())), preferred_element_type=F32)


def dot_tn(a, b):
    return lax.dot_general(a, b, (((0,), (0,)), ((), ())), preferred_element_type=F32)


def lanes_to_row(values):
    total = values[:, 0:128]
    for at in range(128, values.shape[1], 128):
        total = total + values[:, at : at + 128]
    return jnp.sum(total.T, axis=0, keepdims=True)


def row_to_columns(row):
    return jnp.broadcast_to(row, (128, 128)).T


def widen(columns, width):
    return jnp.concatenate([columns] * (width // 128), axis=1)


def kernel(
    seq_n, stride, scatter, x_hbm, ct_hbm, w_hbm, wp_hbm, gain_ref, out_ref, pg_ref, qr2,
    x_ref, w_ref, wp_ref,
    hid, cot, ss, rs, slope, dil, acc_lo, acc_hi, act, hg, y_lo, y_hi, yr_lo, yr_hi, dg, dr_lo, dr_hi,
    part, ps, pr, xf, xs, xr, sg, pn, qs, qr, qs2, send_sem, recv_sem, load_sem,
):
    batch, rows, width = x_ref.shape
    channels = gain_ref.shape[1]
    c = lax.axis_index("chan")
    s = lax.axis_index("seq")
    c1 = c + 1 - 2 * lax.rem(c, 2)
    c2 = lax.rem(c + 2, 4)
    c3 = 3 - c
    peers = (c, c1, c2, c3)
    s1 = s + 1 - 2 * lax.rem(s, 2)
    s2 = lax.rem(s + 2, 4)
    s3 = 3 - s
    has_hi = s + stride < seq_n
    has_lo = s >= stride
    up = lax.rem(s + stride, seq_n)
    down = lax.rem(s - stride + seq_n, seq_n)

    count = [0]
    sent = []

    def copy(src, dst, device):
        k = count[0]
        count[0] += 1
        return pltpu.make_async_remote_copy(
            src_ref=src, dst_ref=dst, send_sem=send_sem.at[k], recv_sem=recv_sem.at[k],
            device_id=device, device_id_type=MESH,
        )

    def push(src, dst, device):
        handle = copy(src, dst, device)
        handle.start()
        sent.append(handle)
        return handle

    def chan_rows(ch):
        return pl.ds(pl.multiple_of(ch * width, width), width)

    loads = [
        pltpu.make_async_copy(src, dst, load_sem.at[i])
        for i, (src, dst) in enumerate(
            ((x_hbm, x_ref), (ct_hbm, cot.at[c]), (w_hbm, w_ref), (wp_hbm, wp_ref))
        )
    ]
    for load in loads:
        load.start()

    barrier = pltpu.get_barrier_semaphore()
    for peer in (c1, c2, c3):
        pl.semaphore_signal(barrier, inc=1, device_id={"chan": peer}, device_id_type=MESH)

    @pl.when(has_hi)
    def _():
        pl.semaphore_signal(barrier, inc=1, device_id={"seq": up}, device_id_type=MESH)

    @pl.when(has_lo)
    def _():
        pl.semaphore_signal(barrier, inc=1, device_id={"seq": down}, device_id_type=MESH)

    if scatter:
        pl.semaphore_signal(barrier, inc=1, device_id={"seq": s1}, device_id_type=MESH)

    loads[0].wait()
    for b in range(batch):
        for at in range(0, rows, 128):
            v = x_ref[b, at : at + 128, :].astype(F32)
            ss[0, :, b * rows + at : b * rows + at + 128] = jnp.broadcast_to(lanes_to_row(v * v), (8, 128))

    loads[1].wait()
    ways = has_hi.astype(jnp.int32) + has_lo.astype(jnp.int32)
    pl.semaphore_wait(barrier, ways + (4 if scatter else 3))

    ss_in = [push(ss.at[0], ss.at[k], {"chan": peers[k]}) for k in (2, 3, 1)]
    cot_in = [[None] * batch for _ in range(4)]
    hid_in = [[None] * batch for _ in range(4)]

    def spread_cot(b):
        cot_in[2][b] = push(cot.at[c, b], cot.at[c, b], {"chan": c2})
        cot_in[1][b] = push(cot.at[c, b], cot.at[c, b], {"chan": c1})

    def relay_cot(b):
        copy_in = cot_in[2][b]
        copy_in.wait_recv()
        cot_in[3][b] = push(cot.at[c2, b], cot.at[c2, b], {"chan": c1})

    spread_cot(0)
    for handle in ss_in:
        handle.wait_recv()
    gain = gain_ref[:, chan_rows(c)]
    for b in range(batch):
        for at in range(0, rows, 128):
            here = slice(b * rows + at, b * rows + at + 128)
            total = ss[0, 0:1, here] + ss[1, 0:1, here] + ss[2, 0:1, here] + ss[3, 0:1, here]
            columns = row_to_columns(lax.rsqrt(total * (1.0 / channels) + epsilon))
            rs[b, at : at + 128, :] = columns
            normed = x_ref[b, at : at + 128, :].astype(F32) * widen(columns, width) * gain
            hid[0, b, at : at + 128, :] = gelu_value(normed).astype(BF16)
        hid_in[2][b] = push(hid.at[0, b], hid.at[2, b], {"chan": c2})
        hid_in[1][b] = push(hid.at[0, b], hid.at[1, b], {"chan": c1})
    for b in range(1, batch):
        spread_cot(b)

    def normed_slope(b):
        for at in range(0, rows, 128):
            normed = x_ref[b, at : at + 128, :].astype(F32) * widen(rs[b, at : at + 128, :], width) * gain
            slope[b, at : at + 128, :] = gelu_slope(normed) * gain

    normed_slope(0)
    relay_cot(0)

    loads[2].wait()
    loads[3].wait()
    halo = [None] * batch
    for b in range(batch):
        for k in range(4):
            if k > 0:
                hid_in[k][b].wait_recv()
            if k == 2:
                hid_in[3][b] = push(hid.at[2, b], hid.at[3, b], {"chan": c1})
            w_rows = chan_rows(peers[k])

            @pl.when(has_hi)
            def _():
                term = dot_nt(w_ref[0, :, w_rows], hid[k, b])
                acc_hi[...] = term if k == 0 else acc_hi[...] + term

            @pl.when(has_lo)
            def _():
                term = dot_nt(w_ref[2, :, w_rows], hid[k, b])
                acc_lo[...] = term if k == 0 else acc_lo[...] + term

        to_hi = copy(y_hi.at[b], yr_lo.at[b], {"seq": up})
        to_lo = copy(y_lo.at[b], yr_hi.at[b], {"seq": down})
        halo[b] = (to_hi, to_lo)

        @pl.when(has_hi)
        def _():
            y_hi[b] = acc_hi[...].astype(BF16)
            to_hi.start()

        @pl.when(has_lo)
        def _():
            y_lo[b] = acc_lo[...].astype(BF16)
            to_lo.start()

        dil[b] = sum(dot_nt(w_ref[1, :, chan_rows(peers[k])], hid[k, b]) for k in range(4))

    def hidden_grad(b):
        cot_in[1][b].wait_recv()
        cot_in[3][b].wait_recv()
        hg[b] = sum(dot_nt(wp_ref[:, j * width : (j + 1) * width], cot[j, b]) for j in range(4))

    hidden_grad(0)
    for b in range(1, batch):
        normed_slope(b)
    if batch > 1:
        relay_cot(1)

    back = [None] * batch
    for b in range(batch):
        to_hi, to_lo = halo[b]

        @pl.when(has_lo)
        def _():
            to_hi.wait_recv()
            dil[b] += yr_lo[b].astype(F32)

        @pl.when(has_hi)
        def _():
            to_lo.wait_recv()
            dil[b] += yr_hi[b].astype(F32)

        if b > 0:
            hidden_grad(b)
        value = dil[b]
        dg[b] = (hg[b] * gelu_slope(value)).astype(BF16)
        g_hi = copy(dg.at[b], dr_lo.at[b], {"seq": up})
        g_lo = copy(dg.at[b], dr_hi.at[b], {"seq": down})
        back[b] = (g_hi, g_lo)

        @pl.when(has_hi)
        def _():
            g_hi.start()

        @pl.when(has_lo)
        def _():
            g_lo.start()

        if b + 2 < batch:
            relay_cot(b + 2)
        act[b] = gelu_value(value).astype(BF16)

    def point_grad(j):
        return sum(dot_nn(act[b], cot[j, b]) for b in range(batch))

    first = [None] * batch
    cross = [None] * batch

    def partial_grads(b):
        g_hi, g_lo = back[b]

        @pl.when(has_hi)
        def _():
            g_lo.wait_recv()

        @pl.when(has_lo)
        def _():
            g_hi.wait_recv()

        part[...] = dot_tn(dg[b], w_ref[1])

        @pl.when(has_hi)
        def _():
            part[...] += dot_tn(dr_hi[b], w_ref[0])

        @pl.when(has_lo)
        def _():
            part[...] += dot_tn(dr_lo[b], w_ref[2])

        ps[b, 1] = part[:, chan_rows(c3)].astype(BF16)
        cross[b] = push(ps.at[b, 1], pr.at[b, 1], {"chan": c1})
        ps[b, 0] = part[:, chan_rows(c1)].astype(BF16)
        first[b] = push(ps.at[b, 0], pr.at[b, 0], {"chan": c1})
        sg[b] = part[:, chan_rows(c)]
        xf[b] = part[:, chan_rows(c2)]

    def cross_over(b):
        cross[b].wait_recv()
        xs[b] = (xf[b] + pr[b, 1].astype(F32)).astype(BF16)
        cross[b] = push(xs.at[b], xr.at[b], {"chan": c2})

    partial_grads(0)
    if scatter:
        qs[0] = point_grad(s1).astype(BF16)
        qs[1] = point_grad(s3).astype(BF16)
        q1 = push(qs, qr, {"seq": s1})
    cross_over(0)
    for b in range(1, batch):
        partial_grads(b)
        if scatter and b == batch - 1:
            pg_ref[...] = point_grad(s)
        if b > 1:
            cross_over(b - 1)
    if batch > 1:
        cross_over(batch - 1)
    if scatter:
        q1.wait_recv()
        qs2[...] = (point_grad(s2) + qr[1].astype(F32)).astype(BF16)
        q2 = push(qs2, qr2, {"seq": s2})
        pg_ref[...] += qr[0].astype(F32)
    else:
        for j in range(4):
            pg_ref[:, j * width : (j + 1) * width] = point_grad(j)
        qr2[...] = jnp.zeros(qr2.shape, BF16)

    inner = [None] * batch
    for b in range(batch):
        first[b].wait_recv()
        cross[b].wait_recv()
        for at in range(0, rows, 128):
            here = slice(at, at + 128)
            raw = sg[b, here, :] + pr[b, 0, here, :].astype(F32) + xr[b, here, :].astype(F32)
            scaled = raw * slope[b, here, :]
            sg[b, here, :] = scaled
            unit = x_ref[b, here, :].astype(F32) * widen(rs[b, here, :], width)
            pn[b, 0, :, here] = jnp.broadcast_to(lanes_to_row(scaled * unit), (8, 128))
        inner[b] = [push(pn.at[b, 0], pn.at[b, k], {"chan": peers[k]}) for k in (2, 3, 1)]
    if scatter:
        q2.wait_recv()
    for b in range(batch):
        for handle in inner[b]:
            handle.wait_recv()
        for at in range(0, rows, 128):
            here = slice(at, at + 128)
            total = pn[b, 0, 0:1, here] + pn[b, 1, 0:1, here] + pn[b, 2, 0:1, here] + pn[b, 3, 0:1, here]
            mean = widen(row_to_columns(total * (1.0 / channels)), width)
            scale = widen(rs[b, here, :], width)
            unit = x_ref[b, here, :].astype(F32) * scale
            out_ref[b, here, :] = scale * (sg[b, here, :] - unit * mean)

    for handle in sent:
        handle.wait_send()
    for b in range(batch):
        for hi, lo in (halo[b], back[b]):

            @pl.when(has_hi)
            def _():
                hi.wait_send()

            @pl.when(has_lo)
            def _():
                lo.wait_send()


def per_device(seq_n, inputs, cotangent, dilated_weight, w_point, norm_gain):
    stride = DILATION_STEP // inputs.shape[1]
    rows, width = 128, inputs.shape[2]
    batch = inputs.shape[0] * inputs.shape[1] // rows
    cut = (batch, rows, width)
    channels = norm_gain.shape[0]
    units = w_point.shape[1]
    scatter = seq_n * width == channels
    wide = lambda *lead: pltpu.VMEM((*lead, rows, width), BF16)
    thin = lambda *lead: pltpu.VMEM((*lead, units, rows), BF16)
    thin32 = lambda *lead: pltpu.VMEM((*lead, units, rows), F32)
    pg_rows = width if scatter else channels
    block = lambda *lead: pltpu.VMEM((*lead, units, width), BF16)
    vmem = pl.BlockSpec(memory_space=pltpu.VMEM)
    hbm = pl.BlockSpec(memory_space=pltpu.HBM)
    branch_grad, point_grad, point_rest = pl.pallas_call(
        functools.partial(kernel, seq_n, stride, scatter),
        out_shape=(
            jax.ShapeDtypeStruct(cut, F32),
            jax.ShapeDtypeStruct((units, pg_rows), F32),
            jax.ShapeDtypeStruct((units, width), BF16),
        ),
        in_specs=[hbm] * 4 + [vmem],
        out_specs=(vmem, vmem, vmem),
        scratch_shapes=[
            wide(batch),
            pltpu.VMEM((3, units, channels), BF16),
            pltpu.VMEM((units, channels), BF16),
            wide(4, batch),
            wide(4, batch),
            pltpu.VMEM((4, 8, batch * rows), F32),
            pltpu.VMEM((batch, rows, 128), F32),
            pltpu.VMEM((batch, rows, width), F32),
            thin32(batch),
            thin32(),
            thin32(),
            thin(batch),
            thin32(batch),
            thin(batch), thin(batch), thin(batch), thin(batch),
            thin(batch), thin(batch), thin(batch),
            pltpu.VMEM((rows, channels), F32),
            wide(batch, 2), wide(batch, 2),
            pltpu.VMEM((batch, rows, width), F32),
            wide(batch), wide(batch),
            pltpu.VMEM((batch, rows, width), F32),
            pltpu.VMEM((batch, 4, 8, rows), F32),
            block(2), block(2), block(),
            pltpu.SemaphoreType.DMA((N_SEMS,)),
            pltpu.SemaphoreType.DMA((N_SEMS,)),
            pltpu.SemaphoreType.DMA((4,)),
        ],
        compiler_params=pltpu.CompilerParams(
            collective_id=0, has_side_effects=True, vmem_limit_bytes=61 * 1024 * 1024
        ),
    )(
        inputs.reshape(cut), cotangent.reshape(cut), dilated_weight.transpose(0, 2, 1), w_point.T, norm_gain.reshape(1, channels)
    )
    input_grad = (cotangent.astype(F32) + branch_grad.reshape(cotangent.shape)).astype(BF16)
    if scatter:
        point_grad = (point_grad + point_rest.astype(F32)).T
    else:
        point_grad = point_grad.T
        point_grad = lax.psum_scatter(point_grad, "seq", scatter_dimension=0, tiled=True)
    return (input_grad, point_grad)


def solution(mesh):
    placed = (
        P("grp", "seq", "chan"),
        P("grp", "seq", "chan"),
        P(None, None, "chan"),
        P(None, "chan"),
        P(),
    )
    return jax.shard_map(
        functools.partial(per_device, mesh.shape["seq"]),
        mesh=mesh,
        in_specs=placed,
        out_specs=(P("grp", "seq", "chan"), P(("grp", "seq"), "chan")),
        check_vma=False,
    )
```
